512 devices in a mesh: fsdp: 16 (over x_hi, y), tp: 32 (over z, x_lo, core).
Axes of the slice: x: 4 (x_hi: 2, x_lo: 2; x = x_hi * 2 + x_lo), y: 8, z: 8, core: 2. Of those that a mesh axis runs over, the one named last changes fastest.
Arguments:
- attention_output: bfloat16 [3072, 8192], P('fsdp', 'tp'), may hold values from -6 to 6
- output_weight: bfloat16 [8192, 8192], P('tp', 'fsdp'), may hold values from -0.0625 to 0.0625
- adapter_down_maps: bfloat16 [64, 16, 8192], P('fsdp', None, 'tp'), may hold values from -0.0625 to 0.0625
- adapter_up_maps: bfloat16 [64, 16, 8192], P('fsdp', None, 'tp'), may hold values from -1.5 to 1.5
- adapter_index: int32 [16, 6], P('fsdp'), may hold values from 0 to 63
- lengths: int32 [16, 6], P('fsdp'), may hold values from 1 to 32
- cotangent: bfloat16 [3072, 8192], P('fsdp', 'tp'), may hold values from -6 to 6
Outputs:
- mixed: bfloat16 [3072, 8192], P('fsdp', 'tp')
- input_gradient: bfloat16 [3072, 8192], P('fsdp', 'tp')
- grad_down: float32 [64, 16, 8192], P('fsdp', None, 'tp')
- grad_up: float32 [64, 16, 8192], P('fsdp', None, 'tp')
The draws below stay inside these ranges and needn't reach their ends.
All inputs are finite; a program needn't handle non-finite values.
Results may differ from the reference program's by a relative error of at most 0.015.
Values may be sent and summed in bfloat16 or wider, within the bound.
No kernel may reach another device: no remote copies, remote signals or barrier semaphores. Data moves between devices by JAX's collectives and lax.ppermute only.
A program may use at most 64 MiB of HBM per device.

```python
import jax
import jax.numpy as jnp
from jax import lax

MODEL_WIDTH = 8192
ADAPTER_RANK = 16
SLOTS = 6
SLOT_LEN = 32
ADAPTER_COUNT = 64
GROUPS = 16
TOKENS = 3072
N_TP = 32


def plant(drawn, stream_key, least, largest):
    longest = drawn.shape.index(max(drawn.shape))
    spots = []
    for shift in (0, 1):
        where = [jax.random.randint(jax.random.fold_in(stream_key, axis), (), 0, length) for axis, length in enumerate(drawn.shape)]
        where[longest] = (where[longest] + shift) % drawn.shape[longest]
        spots.append(tuple(where))
    return drawn.at[spots[0]].set(least).at[spots[1]].set(largest)


def shard_levels(own_key, dims, shards, least, largest):
    loudness = 1.0
    for position, blocks in shards:
        steps = jax.random.uniform(jax.random.fold_in(jax.random.fold_in(own_key, 6), position), (blocks,), jnp.float32, least / len(shards), largest / len(shards))
        loudness = loudness * jnp.repeat(jnp.exp(steps), dims[position] // blocks).reshape((-1,) + (1,) * (len(dims) - 1 - position))
    return loudness


def noise(own_key, dims, deviation, most, pieces=(), kind=jnp.bfloat16):
    values = deviation * jax.random.normal(own_key, dims, jnp.float32)
    if pieces:
        values = values * shard_levels(own_key, dims, pieces, -0.22, 0.18)
    return jnp.clip(values, -most, most).astype(kind)


def setup_inputs(seed: int = 0) -> dict:
    arg_keys = jax.random.split(jax.random.key(seed), 8)
    attention_output = noise(arg_keys[0], (TOKENS, MODEL_WIDTH), 1.0, 6.0, ((0, 16), (1, 32)))
    output_weight = noise(arg_keys[1], (MODEL_WIDTH, MODEL_WIDTH), MODEL_WIDTH ** -0.5, 0.0625, ((0, 32), (1, 16)))
    adapter_down_maps = noise(arg_keys[2], (ADAPTER_COUNT, ADAPTER_RANK, MODEL_WIDTH), MODEL_WIDTH ** -0.5, 0.0625, ((0, 16), (2, 32)))
    adapter_up_maps = noise(arg_keys[3], (ADAPTER_COUNT, ADAPTER_RANK, MODEL_WIDTH), ADAPTER_RANK ** -0.5, 1.5, ((0, 16), (2, 32)))
    adapter_index = plant(jax.random.randint(arg_keys[4], (GROUPS, SLOTS), 0, ADAPTER_COUNT), jax.random.fold_in(arg_keys[4], 1), 0, ADAPTER_COUNT - 1).astype(jnp.int32)
    lengths = plant(jax.random.randint(arg_keys[5], (GROUPS, SLOTS), 1, SLOT_LEN + 1), jax.random.fold_in(arg_keys[5], 1), 1, SLOT_LEN).astype(jnp.int32)
    cotangent = noise(arg_keys[6], (TOKENS, MODEL_WIDTH), 1.0, 6.0, ((0, 16), (1, 32)))
    return dict(attention_output=attention_output, output_weight=output_weight, adapter_down_maps=adapter_down_maps, adapter_up_maps=adapter_up_maps, adapter_index=adapter_index, lengths=lengths, cotangent=cotangent)


adapter_scale = 2.0


def to_wire(value):
    rounded = lax.optimization_barrier(value.astype(jnp.bfloat16))
    return rounded.astype(jnp.float32)


def reference(attention_output, output_weight, adapter_down_maps, adapter_up_maps, adapter_index, lengths, cotangent):
    groups = adapter_index.shape[0]
    token_count = attention_output.shape[0]
    feature_width = MODEL_WIDTH // N_TP
    highest_precision = lax.Precision.HIGHEST
    x_blocks = attention_output.reshape(token_count, N_TP, feature_width).transpose(1, 0, 2)
    w_blocks = output_weight.reshape(N_TP, feature_width, MODEL_WIDTH)

    def add_block(running, item_pair):
        part = jnp.dot(item_pair[0], item_pair[1], preferred_element_type=jnp.float32)
        return running + to_wire(part), None

    frozen_product, _ = lax.scan(add_block, jnp.zeros((token_count, MODEL_WIDTH), jnp.float32), (x_blocks, w_blocks))
    slot_index = adapter_index.reshape(-1)
    selected_down = adapter_down_maps[slot_index].astype(jnp.float32)
    selected_up = adapter_up_maps[slot_index].astype(jnp.float32)
    slot_rows = attention_output.reshape(groups * SLOTS, SLOT_LEN, MODEL_WIDTH).astype(jnp.float32)
    rank_middle = jnp.einsum('ucd,utd->uct', slot_rows, selected_down, precision=highest_precision).astype(jnp.bfloat16)
    adapter_output = jnp.einsum('jae,jeq->jaq', rank_middle.astype(jnp.float32), selected_up, precision=highest_precision)
    mixed = (frozen_product + adapter_scale * adapter_output.reshape(token_count, MODEL_WIDTH)).astype(jnp.bfloat16)
    positions = jnp.arange(SLOT_LEN, dtype=jnp.int32)
    live_mask = (positions[None, None, :] < lengths[:, :, None]).reshape(groups * SLOTS, SLOT_LEN)
    grad_out = cotangent.reshape(groups * SLOTS, SLOT_LEN, MODEL_WIDTH) * live_mask[:, :, None].astype(jnp.bfloat16)
    gradient_float = grad_out.astype(jnp.float32)
    middle_gradient = (adapter_scale * jnp.einsum('ucd,utd->uct', gradient_float, selected_up, precision=highest_precision)).astype(jnp.bfloat16)
    slot_up_map = adapter_scale * jnp.einsum('gnx,gnu->gxu', rank_middle.astype(jnp.float32), gradient_float, precision=highest_precision)
    down_slot = jnp.einsum('gnx,gnu->gxu', middle_gradient.astype(jnp.float32), slot_rows, precision=highest_precision)
    one_hot = (adapter_index[:, :, None] == jnp.arange(ADAPTER_COUNT, dtype=jnp.int32)[None, None, :]).astype(jnp.float32)

    def add_group(totals, item_group):
        hot_rows, up_terms, down_terms = item_group
        part_up = jnp.einsum('sa,srf->arf', hot_rows, up_terms, precision=highest_precision)
        part_down = jnp.einsum('sa,srf->arf', hot_rows, down_terms, precision=highest_precision)
        return (totals[0] + to_wire(part_down), totals[1] + to_wire(part_up)), None

    zeros_grad = jnp.zeros((ADAPTER_COUNT, ADAPTER_RANK, MODEL_WIDTH), jnp.float32)
    sums, _ = lax.scan(add_group, (zeros_grad, zeros_grad),
                       (one_hot, slot_up_map.reshape(groups, SLOTS, ADAPTER_RANK, MODEL_WIDTH), down_slot.reshape(groups, SLOTS, ADAPTER_RANK, MODEL_WIDTH)))
    backward_pass = jnp.dot(grad_out.reshape(token_count, MODEL_WIDTH), output_weight.T, preferred_element_type=jnp.float32)
    adapter_backward = jnp.einsum('jae,jeq->jaq', middle_gradient.astype(jnp.float32), selected_down, precision=highest_precision)
    input_gradient = (backward_pass + adapter_backward.reshape(token_count, MODEL_WIDTH)).astype(jnp.bfloat16)
    return mixed, input_gradient, sums[0], sums[1]
```

```python
import jax
import jax.numpy as jnp
from jax import lax
from jax.experimental import pallas as pl
from jax.experimental.pallas import tpu as pltpu
from jax.sharding import PartitionSpec as P

AXES = ("fsdp", "tp")
SCALE = 2.0
SLOTS = 6
SLOT_LEN = 32
RANK = 16
RING = 8
BF16 = jnp.bfloat16
F32 = jnp.float32


def flat(xh, y, z, xl, c):
    return (xh * RING + y) * 4 * RING + z * 4 + xl * 2 + c


DEVICES = [
    (xh, y, z, xl, c)
    for xh in range(2)
    for y in range(RING)
    for z in range(RING)
    for xl in range(2)
    for c in range(2)
]


def pairs(move):
    return [(flat(*d), flat(*move(*d))) for d in DEVICES]


SWAP_CORE = pairs(lambda xh, y, z, xl, c: (xh, y, z, xl, 1 - c))
SWAP_LOW = pairs(lambda xh, y, z, xl, c: (xh, y, z, 1 - xl, c))
SWAP_HIGH = pairs(lambda xh, y, z, xl, c: (1 - xh, y, z, xl, c))
SWAP_Z = [pairs(lambda xh, y, z, xl, c, k=k: (xh, y, z ^ k, xl, c)) for k in (1, 2, 4)]


def to_blocks(a):
    def move(xh, y, z, xl, c):
        if c == 0:
            return (xh, y, z, xl ^ a, c)
        return (xh, (2 * z + xl) % RING, y, a ^ (z >> 2), c)

    return pairs(move)


def from_blocks(a):
    def move(xh, y, z, xl, c):
        if c == 1:
            return (xh, y, z, xl ^ a, c)
        return (xh, z, 4 * (xl ^ a) + (y >> 1), y & 1, c)

    return pairs(move)


TO_BLOCKS = [to_blocks(a) for a in (0, 1)]
FROM_BLOCKS = [from_blocks(a) for a in (0, 1)]


def along_y(xh, z, xl, c):
    return [flat(xh, k, z, xl, c) for k in range(RING)]


def along_z(xh, y, xl, c):
    return [flat(xh, y, k, xl, c) for k in range(RING)]


OUTER = [(xh, k, xl) for xh in range(2) for k in range(RING) for xl in range(2)]
GROUPS_Y = [along_y(*o, c) for o in OUTER for c in range(2)]
GROUPS_GATHER = [along_y(*o, 0) for o in OUTER] + [along_z(*o, 1) for o in OUTER]
GROUPS_SCATTER = [along_z(*o, 0) for o in OUTER] + [along_y(*o, 1) for o in OUTER]


def permute(value, where):
    return lax.ppermute(value, AXES, where)


def exchange(value, groups):
    return lax.all_to_all(value, AXES, 0, 0, axis_index_groups=groups, tiled=True)


def product_kernel(core_ref, rows_ref, near_ref, far_ref, out_ref):
    half = near_ref.shape[0]

    @pl.when(core_ref[0] == 0)
    def _():
        out_ref[...] = (
            jnp.dot(rows_ref[:, :half], near_ref[...], preferred_element_type=F32)
            + jnp.dot(rows_ref[:, half:], far_ref[...], preferred_element_type=F32)
        ).astype(out_ref.dtype)

    @pl.when(core_ref[0] != 0)
    def _():
        contract = (((1,), (1,)), ((), ()))
        for k, ref in enumerate((near_ref, far_ref)):
            out_ref[:, k * half : (k + 1) * half] = lax.dot_general(
                rows_ref[...], ref[...], contract, preferred_element_type=F32
            ).astype(out_ref.dtype)


def product(core, rows, near, far):
    count, width = rows.shape
    tile = count // 4
    whole = lambda i: (0, 0)
    return pl.pallas_call(
        product_kernel,
        grid=(count // tile,),
        in_specs=[
            pl.BlockSpec(memory_space=pltpu.SMEM),
            pl.BlockSpec((tile, width), lambda i: (i, 0)),
            pl.BlockSpec(near.shape, whole),
            pl.BlockSpec(far.shape, whole),
        ],
        out_specs=pl.BlockSpec((tile, width), lambda i: (i, 0)),
        out_shape=jax.ShapeDtypeStruct((count, width), BF16),
        compiler_params=pltpu.CompilerParams(vmem_limit_bytes=24 * 1024 * 1024),
        cost_estimate=pl.CostEstimate(
            flops=2 * count * width * width, bytes_accessed=4 * count * width + 2 * width * width, transcendentals=0
        ),
    )(core, rows, near, far)


def body(attention_output, output_weight, down_maps, up_maps, adapter_index, lengths, cotangent):
    fsdp, tp = lax.axis_index("fsdp"), lax.axis_index("tp")
    xh, z, xl, c = fsdp // RING, tp // 4, (tp // 2) % 2, tp % 2
    first = c == 0
    tokens, width = attention_output.shape
    half = tokens // 2
    own = down_maps.shape[0]

    slots = adapter_index[0]
    other_slots = permute(adapter_index, SWAP_HIGH)[0]
    table = jnp.stack([down_maps, up_maps])
    tables = exchange(jnp.broadcast_to(table[None], (RING,) + table.shape).reshape(RING, -1, width), GROUPS_Y)
    tables = tables.reshape(RING, 2, own, RANK, width)

    positions = lax.iota(jnp.int32, SLOT_LEN)
    live = (positions[None, :] < lengths[0][:, None]).astype(BF16)
    grad_out = (cotangent.reshape(SLOTS, SLOT_LEN, width) * live[:, :, None]).reshape(tokens, width)
    mine = jnp.where(first, attention_output, grad_out)
    theirs = permute(jnp.where(first, grad_out, attention_output), SWAP_CORE)
    pair = jnp.where(first, jnp.concatenate([mine, theirs], 1), jnp.concatenate([theirs, mine], 1))
    side = jnp.where(first, xl, z >> 2)
    top, bottom = pair[:half], pair[half:]
    got = [
        permute(jnp.where(side == 0, top, bottom), TO_BLOCKS[0]),
        permute(jnp.where(side == 0, bottom, top), TO_BLOCKS[1]),
    ]
    flip = (xh ^ xl) == 1
    rows_x = jnp.concatenate([got[0][:, :width], got[1][:, :width], got[0][:, width:], got[1][:, width:]], 1)
    rows_g = jnp.concatenate([jnp.where(flip, got[1], got[0]), jnp.where(flip, got[0], got[1])], 1)
    rows = jnp.where(first, rows_x, rows_g)
    gathered = exchange(jnp.broadcast_to(rows[None], (RING,) + rows.shape), GROUPS_GATHER)

    block = jnp.concatenate([output_weight, permute(output_weight, SWAP_LOW)], 0)
    near = jnp.concatenate([block, permute(block, SWAP_HIGH)], 1)
    far = permute(near, SWAP_CORE)

    partial_value = product(c.reshape(1), gathered.reshape(RING * half, 4 * width), near, far)
    spread = exchange(partial_value.reshape(RING, half, 4 * width), GROUPS_SCATTER)
    total = jnp.sum(spread.astype(F32), 0).astype(BF16)

    def pick(which):
        local = which % (RING * own)
        return tables[local // own, :, local % own]

    high = slots // (RING * own)
    other_high = other_slots // (RING * own)
    give = jnp.where((other_high == xh)[:, None, None, None], pick(other_slots), 0)
    take = permute(give.reshape(-1, width), SWAP_HIGH).reshape(SLOTS, 2, RANK, width)
    chosen = jnp.where((high == xh)[:, None, None, None], pick(slots), take)
    chosen_down = chosen[:, 0].reshape(SLOTS * RANK, width)
    chosen_up = chosen[:, 1].reshape(SLOTS * RANK, width)

    own_slot = (lax.iota(jnp.int32, tokens)[None, :] // SLOT_LEN) == lax.iota(jnp.int32, SLOTS)[:, None]
    contract = (((1,), (1,)), ((), ()))

    def rank_product(maps, values):
        every = lax.dot_general(maps, values, contract, preferred_element_type=F32)
        every = every.reshape(SLOTS, RANK, tokens)
        return jnp.sum(jnp.where(own_slot[:, None, :], every, 0.0), 0)

    sums = jnp.concatenate(
        [rank_product(chosen_down, attention_output), SCALE * rank_product(chosen_up, grad_out)], 0
    )
    for where in (SWAP_CORE, SWAP_LOW, *SWAP_Z):
        sums = sums + permute(sums, where)
    ranks = sums.astype(BF16)

    def per_slot(value):
        spread_out = jnp.where(own_slot[:, None, :], value[None], jnp.zeros((), BF16))
        return spread_out.reshape(SLOTS * RANK, tokens)

    middle, grad_middle = per_slot(ranks[:RANK]), per_slot(ranks[RANK:])

    up_terms = (SCALE * jnp.dot(middle, grad_out, preferred_element_type=F32)).astype(BF16)
    down_terms = jnp.dot(grad_middle, attention_output, preferred_element_type=F32).astype(BF16)
    terms = jnp.stack([down_terms, up_terms]).reshape(2, SLOTS, RANK * width)
    away = permute(terms.reshape(2 * SLOTS * RANK, width), SWAP_HIGH).reshape(terms.shape)
    adapters = lax.iota(jnp.int32, RING * own) + xh * (RING * own)
    hot = jnp.concatenate(
        [(adapters[:, None] == slots[None, :]), (adapters[:, None] == other_slots[None, :])], 1
    ).astype(BF16)
    both = jnp.concatenate([terms, away], 1)
    owned = jnp.einsum("as,ksw->akw", hot, both, preferred_element_type=F32).astype(BF16)
    owned = owned.reshape(RING, own * 2 * RANK, width)
    grads = jnp.sum(exchange(owned, GROUPS_Y).astype(F32), 0).reshape(own, 2, RANK, width)

    quarters = total.reshape(half, 2, 2, width)
    halves = total.reshape(half, 2, 2 * width)
    out = []
    for a in (0, 1):
        forward = jnp.where(flip, halves[:, 1 - a], halves[:, a])
        backward = quarters[:, :, a].reshape(half, 2 * width)
        out.append(permute(jnp.where(first, forward, backward), FROM_BLOCKS[a]))
    back = jnp.where(first, z >> 2, xl)
    both_halves = jnp.concatenate(
        [jnp.where(back == 0, out[0], out[1]), jnp.where(back == 0, out[1], out[0])], 0
    )
    kept = both_halves[:, :width]
    swapped = permute(both_halves[:, width:], SWAP_CORE)
    base = jnp.where(first, kept, swapped).astype(F32)
    frozen_gradient = jnp.where(first, swapped, kept).astype(F32)

    tokens_first = (((0,), (0,)), ((), ()))
    mixed = base + SCALE * lax.dot_general(middle, chosen_up, tokens_first, preferred_element_type=F32)
    input_gradient = frozen_gradient + lax.dot_general(
        grad_middle, chosen_down, tokens_first, preferred_element_type=F32
    )
    return mixed.astype(BF16), input_gradient.astype(BF16), grads[:, 0], grads[:, 1]


def solution(mesh):
    maps = P("fsdp", None, "tp")
    flat_spec = P("fsdp", "tp")
    return jax.shard_map(
        body,
        mesh=mesh,
        in_specs=(flat_spec, P("tp", "fsdp"), maps, maps, P("fsdp", None), P("fsdp", None), flat_spec),
        out_specs=(flat_spec, flat_spec, maps, maps),
        check_vma=False,
    )
```

```python
import jax
import jax.numpy as jnp
from jax import lax
from jax.experimental import pallas as pl
from jax.experimental.pallas import tpu as pltpu
from jax.sharding import PartitionSpec as P

AXES = ("fsdp", "tp")
SCALE = 2.0
SLOTS = 6
SLOT_LEN = 32
RANK = 16
RING = 8
BF16 = jnp.bfloat16
F32 = jnp.float32


def flat(xh, y, z, xl, c):
    return (xh * RING + y) * 4 * RING + z * 4 + xl * 2 + c


DEVICES = [
    (xh, y, z, xl, c)
    for xh in range(2)
    for y in range(RING)
    for z in range(RING)
    for xl in range(2)
    for c in range(2)
]


def pairs(move):
    return [(flat(*d), flat(*move(*d))) for d in DEVICES]


SWAP_CORE = pairs(lambda xh, y, z, xl, c: (xh, y, z, xl, 1 - c))
SWAP_LOW = pairs(lambda xh, y, z, xl, c: (xh, y, z, 1 - xl, c))
SWAP_HIGH = pairs(lambda xh, y, z, xl, c: (1 - xh, y, z, xl, c))


def to_blocks(a):
    def move(xh, y, z, xl, c):
        if c == 0:
            return (xh, y, z, xl ^ a, c)
        return (xh, (2 * z + xl) % RING, y, a ^ (z >> 2), c)

    return pairs(move)


def from_blocks(a):
    def move(xh, y, z, xl, c):
        if c == 1:
            return (xh, y, z, xl ^ a, c)
        return (xh, (z - y) % RING, 4 * (xl ^ a) + (y >> 1), y & 1, c)

    return pairs(move)


TO_BLOCKS = [to_blocks(a) for a in (0, 1)]
FROM_BLOCKS = [from_blocks(a) for a in (0, 1)]


def along_y(xh, z, xl, c):
    return [flat(xh, k, z, xl, c) for k in range(RING)]


def along_z(xh, y, xl, c, turn=0):
    return [flat(xh, y, (k + turn) % RING, xl, c) for k in range(RING)]


OUTER = [(xh, k, xl) for xh in range(2) for k in range(RING) for xl in range(2)]
GROUPS_Y = [along_y(*o, c) for o in OUTER for c in range(2)]
GROUPS_Z = [along_z(*o, c) for o in OUTER for c in range(2)]
GROUPS_GATHER = [along_y(*o, 0) for o in OUTER] + [along_z(*o, 1) for o in OUTER]
GROUPS_SCATTER = [along_z(*o, 0, o[1]) for o in OUTER] + [along_y(*o, 1) for o in OUTER]


def permute(value, where):
    return lax.ppermute(value, AXES, where)


def exchange(value, groups):
    return lax.all_to_all(value, AXES, 0, 0, axis_index_groups=groups, tiled=True)


def after(value, *others):
    return lax.optimization_barrier((value, *others))[0]


def product_kernel(core_ref, rows_ref, near_ref, far_ref, out_ref):
    half = near_ref.shape[0]

    @pl.when(core_ref[0] == 0)
    def _():
        out_ref[...] = (
            jnp.dot(rows_ref[:, :half], near_ref[...], preferred_element_type=F32)
            + jnp.dot(rows_ref[:, half:], far_ref[...], preferred_element_type=F32)
        ).astype(out_ref.dtype)

    @pl.when(core_ref[0] != 0)
    def _():
        contract = (((1,), (1,)), ((), ()))
        for k, ref in enumerate((near_ref, far_ref)):
            out_ref[:, k * half : (k + 1) * half] = lax.dot_general(
                rows_ref[...], ref[...], contract, preferred_element_type=F32
            ).astype(out_ref.dtype)


def product(core, rows, near, far):
    count, width = rows.shape
    tile = count // 4
    whole = lambda i: (0, 0)
    return pl.pallas_call(
        product_kernel,
        grid=(count // tile,),
        in_specs=[
            pl.BlockSpec(memory_space=pltpu.SMEM),
            pl.BlockSpec((tile, width), lambda i: (i, 0)),
            pl.BlockSpec(near.shape, whole),
            pl.BlockSpec(far.shape, whole),
        ],
        out_specs=pl.BlockSpec((tile, width), lambda i: (i, 0)),
        out_shape=jax.ShapeDtypeStruct((count, width), BF16),
        compiler_params=pltpu.CompilerParams(vmem_limit_bytes=24 * 1024 * 1024),
        cost_estimate=pl.CostEstimate(
            flops=2 * count * width * width, bytes_accessed=4 * count * width + 2 * width * width, transcendentals=0
        ),
    )(core, rows, near, far)


def body(attention_output, output_weight, down_maps, up_maps, adapter_index, lengths, cotangent):
    fsdp, tp = lax.axis_index("fsdp"), lax.axis_index("tp")
    xh, z, xl, c = fsdp // RING, tp // 4, (tp // 2) % 2, tp % 2
    first = c == 0
    tokens, width = attention_output.shape
    half = tokens // 2
    own = down_maps.shape[0]

    slots = adapter_index[0]
    table = jnp.stack([down_maps, up_maps])
    tables = exchange(jnp.broadcast_to(table[None], (RING,) + table.shape).reshape(RING, -1, width), GROUPS_Y)
    tables = tables.reshape(RING, 2, own, RANK, width)

    positions = lax.iota(jnp.int32, SLOT_LEN)
    live = (positions[None, :] < lengths[0][:, None]).astype(BF16)
    grad_out = (cotangent.reshape(SLOTS, SLOT_LEN, width) * live[:, :, None]).reshape(tokens, width)
    mine = jnp.where(first, attention_output, grad_out)
    theirs = permute(jnp.where(first, grad_out, attention_output), SWAP_CORE)
    pair = jnp.where(first, jnp.concatenate([mine, theirs], 1), jnp.concatenate([theirs, mine], 1))
    other_slots = permute(after(adapter_index, pair), SWAP_HIGH)[0]
    near_rows = permute(after(output_weight, pair), SWAP_LOW)
    side = jnp.where(first, xl, z >> 2)
    top, bottom = pair[:half], pair[half:]
    got = [
        permute(jnp.where(side == 0, top, bottom), TO_BLOCKS[0]),
        permute(jnp.where(side == 0, bottom, top), TO_BLOCKS[1]),
    ]
    flip = (xh ^ xl) == 1
    rows_x = jnp.concatenate([got[0][:, :width], got[1][:, :width], got[0][:, width:], got[1][:, width:]], 1)
    rows_g = jnp.concatenate([jnp.where(flip, got[1], got[0]), jnp.where(flip, got[0], got[1])], 1)
    rows = jnp.where(first, rows_x, rows_g)
    rows = after(rows, near_rows, tables, other_slots)
    gathered = exchange(jnp.broadcast_to(rows[None], (RING,) + rows.shape), GROUPS_GATHER)

    block = jnp.concatenate([output_weight, near_rows], 0)
    near = jnp.concatenate([block, permute(block, SWAP_HIGH)], 1)
    def pick(which):
        local = which % (RING * own)
        return tables[local // own, :, local % own]

    high = slots // (RING * own)
    other_high = other_slots // (RING * own)
    give = jnp.where((other_high == xh)[:, None, None, None], pick(other_slots), 0)
    take = permute(give.reshape(-1, width), SWAP_HIGH).reshape(SLOTS, 2, RANK, width)
    chosen = jnp.where((high == xh)[:, None, None, None], pick(slots), take)
    chosen_down = chosen[:, 0].reshape(SLOTS * RANK, width)
    chosen_up = chosen[:, 1].reshape(SLOTS * RANK, width)

    own_slot = (lax.iota(jnp.int32, tokens)[None, :] // SLOT_LEN) == lax.iota(jnp.int32, SLOTS)[:, None]
    contract = (((1,), (1,)), ((), ()))

    def rank_product(maps, values):
        every = lax.dot_general(maps, values, contract, preferred_element_type=F32)
        every = every.reshape(SLOTS, RANK, tokens)
        return jnp.sum(jnp.where(own_slot[:, None, :], every, 0.0), 0)

    sums = jnp.concatenate(
        [rank_product(chosen_down, attention_output), SCALE * rank_product(chosen_up, grad_out)], 0
    )
    for where in (SWAP_CORE, SWAP_LOW):
        sums = sums + permute(sums, where)
    far = permute(after(near, sums), SWAP_CORE)
    gathered, sums = lax.optimization_barrier((gathered, sums))
    rank_sums = jnp.sum(exchange(jnp.broadcast_to(sums[None], (RING,) + sums.shape), GROUPS_Z), 0)
    partial_value = product(c.reshape(1), gathered.reshape(RING * half, 4 * width), near, far)
    partial_value = after(partial_value, rank_sums)
    spread = exchange(partial_value.reshape(RING, half, 4 * width), GROUPS_SCATTER)
    total = jnp.sum(spread.astype(F32), 0).astype(BF16)

    ranks = rank_sums.astype(BF16)

    def per_slot(value):
        spread_out = jnp.where(own_slot[:, None, :], value[None], jnp.zeros((), BF16))
        return spread_out.reshape(SLOTS * RANK, tokens)

    middle, grad_middle = per_slot(ranks[:RANK]), per_slot(ranks[RANK:])

    up_terms = (SCALE * jnp.dot(middle, grad_out, preferred_element_type=F32)).astype(BF16)
    down_terms = jnp.dot(grad_middle, attention_output, preferred_element_type=F32).astype(BF16)
    terms = jnp.stack([down_terms, up_terms]).reshape(2, SLOTS, RANK * width)
    away = permute(terms.reshape(2 * SLOTS * RANK, width), SWAP_HIGH).reshape(terms.shape)
    adapters = lax.iota(jnp.int32, RING * own) + xh * (RING * own)
    hot = jnp.concatenate(
        [(adapters[:, None] == slots[None, :]), (adapters[:, None] == other_slots[None, :])], 1
    ).astype(BF16)
    both = jnp.concatenate([terms, away], 1)
    owned = jnp.einsum("as,ksw->akw", hot, both, preferred_element_type=F32).astype(BF16)
    owned = owned.reshape(RING, own * 2 * RANK, width)

    quarters = total.reshape(half, 2, 2, width)
    halves = total.reshape(half, 2, 2 * width)
    sent = []
    for a in (0, 1):
        forward = jnp.where(flip, halves[:, 1 - a], halves[:, a])
        backward = quarters[:, :, a].reshape(half, 2 * width)
        sent.append(jnp.where(first, forward, backward))
    out = [permute(sent[a], FROM_BLOCKS[a]) for a in (0, 1)]
    owned = after(owned, *sent)
    grads = jnp.sum(exchange(owned, GROUPS_Y).astype(F32), 0).reshape(own, 2, RANK, width)
    back = jnp.where(first, z >> 2, xl)
    both_halves = jnp.concatenate(
        [jnp.where(back == 0, out[0], out[1]), jnp.where(back == 0, out[1], out[0])], 0
    )
    kept = both_halves[:, :width]
    swapped = permute(both_halves[:, width:], SWAP_CORE)
    base = jnp.where(first, kept, swapped).astype(F32)
    frozen_gradient = jnp.where(first, swapped, kept).astype(F32)

    tokens_first = (((0,), (0,)), ((), ()))
    mixed = base + SCALE * lax.dot_general(middle, chosen_up, tokens_first, preferred_element_type=F32)
    input_gradient = frozen_gradient + lax.dot_general(
        grad_middle, chosen_down, tokens_first, preferred_element_type=F32
    )
    return mixed.astype(BF16), input_gradient.astype(BF16), grads[:, 0], grads[:, 1]


def solution(mesh):
    maps = P("fsdp", None, "tp")
    flat_spec = P("fsdp", "tp")
    return jax.shard_map(
        body,
        mesh=mesh,
        in_specs=(flat_spec, P("tp", "fsdp"), maps, maps, P("fsdp", None), P("fsdp", None), flat_spec),
        out_specs=(flat_spec, flat_spec, maps, maps),
        check_vma=False,
    )
```

```python
import jax
import jax.numpy as jnp
from jax import lax
from jax.experimental import pallas as pl
from jax.experimental.pallas import tpu as pltpu
from jax.sharding import PartitionSpec as P

AXES = ("fsdp", "tp")
SCALE = 2.0
SLOTS = 6
SLOT_LEN = 32
RANK = 16
RING = 8
BF16 = jnp.bfloat16
F32 = jnp.float32


def flat(xh, y, z, xl, c):
    return (xh * RING + y) * 4 * RING + z * 4 + xl * 2 + c


DEVICES = [
    (xh, y, z, xl, c)
    for xh in range(2)
    for y in range(RING)
    for z in range(RING)
    for xl in range(2)
    for c in range(2)
]


def pairs(move):
    return [(flat(*d), flat(*move(*d))) for d in DEVICES]


SWAP_CORE = pairs(lambda xh, y, z, xl, c: (xh, y, z, xl, 1 - c))
SWAP_LOW = pairs(lambda xh, y, z, xl, c: (xh, y, z, 1 - xl, c))
SWAP_HIGH = pairs(lambda xh, y, z, xl, c: (1 - xh, y, z, xl, c))


def to_blocks(a):
    def move(xh, y, z, xl, c):
        if c == 0:
            return (xh, y, z, xl ^ a, c)
        return (xh, (2 * z + xl) % RING, y, a ^ (z >> 2), c)

    return pairs(move)


def from_blocks(a):
    def move(xh, y, z, xl, c):
        if c == 1:
            return (xh, y, z, xl ^ a, c)
        return (xh, (z - y) % RING, 4 * (xl ^ a) + (y >> 1), y & 1, c)

    return pairs(move)


TO_BLOCKS = [to_blocks(a) for a in (0, 1)]
FROM_BLOCKS = [from_blocks(a) for a in (0, 1)]


def along_y(xh, z, xl, c):
    return [flat(xh, k, z, xl, c) for k in range(RING)]


def along_z(xh, y, xl, c, turn=0):
    return [flat(xh, y, (k + turn) % RING, xl, c) for k in range(RING)]


OUTER = [(xh, k, xl) for xh in range(2) for k in range(RING) for xl in range(2)]
GROUPS_Y = [along_y(*o, c) for o in OUTER for c in range(2)]
GROUPS_Z = [along_z(*o, c) for o in OUTER for c in range(2)]
GROUPS_GATHER = [along_y(*o, 0) for o in OUTER] + [along_z(*o, 1) for o in OUTER]
GROUPS_SCATTER = [along_z(*o, 0, o[1]) for o in OUTER] + [along_y(*o, 1) for o in OUTER]


def permute(value, where):
    return lax.ppermute(value, AXES, where)


def exchange(value, groups):
    return lax.all_to_all(value, AXES, 0, 0, axis_index_groups=groups, tiled=True)


together = lax.optimization_barrier


def product_kernel(core_ref, rows_ref, near_ref, far_ref, out_ref):
    half = near_ref.shape[0]

    @pl.when(core_ref[0] == 0)
    def _():
        out_ref[...] = (
            jnp.dot(rows_ref[:, :half], near_ref[...], preferred_element_type=F32)
            + jnp.dot(rows_ref[:, half:], far_ref[...], preferred_element_type=F32)
        ).astype(out_ref.dtype)

    @pl.when(core_ref[0] != 0)
    def _():
        contract = (((1,), (1,)), ((), ()))
        for k, ref in enumerate((near_ref, far_ref)):
            out_ref[:, k * half : (k + 1) * half] = lax.dot_general(
                rows_ref[...], ref[...], contract, preferred_element_type=F32
            ).astype(out_ref.dtype)


def product(core, rows, near, far):
    count, width = rows.shape
    tile = count // 4
    whole = lambda i: (0, 0)
    return pl.pallas_call(
        product_kernel,
        grid=(count // tile,),
        in_specs=[
            pl.BlockSpec(memory_space=pltpu.SMEM),
            pl.BlockSpec((tile, width), lambda i: (i, 0)),
            pl.BlockSpec(near.shape, whole),
            pl.BlockSpec(far.shape, whole),
        ],
        out_specs=pl.BlockSpec((tile, width), lambda i: (i, 0)),
        out_shape=jax.ShapeDtypeStruct((count, width), BF16),
        compiler_params=pltpu.CompilerParams(vmem_limit_bytes=24 * 1024 * 1024),
        cost_estimate=pl.CostEstimate(
            flops=2 * count * width * width, bytes_accessed=4 * count * width + 2 * width * width, transcendentals=0
        ),
    )(core, rows, near, far)


def body(attention_output, output_weight, down_maps, up_maps, adapter_index, lengths, cotangent):
    fsdp, tp = lax.axis_index("fsdp"), lax.axis_index("tp")
    xh, z, xl, c = fsdp // RING, tp // 4, (tp // 2) % 2, tp % 2
    first = c == 0
    tokens, width = attention_output.shape
    half = tokens // 2
    own = down_maps.shape[0]

    slots = adapter_index[0]

    positions = lax.iota(jnp.int32, SLOT_LEN)
    live = (positions[None, :] < lengths[0][:, None]).astype(BF16)
    live = live.reshape(tokens, 1)
    grad_out = cotangent * live
    forward = jnp.concatenate([attention_output, down_maps.reshape(-1, width)], 0)
    backward = jnp.concatenate([cotangent, up_maps.reshape(-1, width)], 0)
    mine = jnp.where(first, forward, backward)
    theirs = permute(jnp.where(first, backward, forward), SWAP_CORE)
    pair = jnp.where(first, jnp.concatenate([mine, theirs], 1), jnp.concatenate([theirs, mine], 1))
    pair, table = pair[:tokens] * jnp.where(first, jnp.ones((), BF16), live), pair[tokens:]

    tables = exchange(jnp.broadcast_to(table[None], (RING,) + table.shape), GROUPS_Y)
    tables = tables.reshape(RING, own, RANK, 2 * width)
    side = jnp.where(first, xl, z >> 2)
    top, bottom = pair[:half], pair[half:]
    got = [
        permute(jnp.where(side == 0, top, bottom), TO_BLOCKS[0]),
        permute(jnp.where(side == 0, bottom, top), TO_BLOCKS[1]),
    ]
    flip = (xh ^ xl) == 1
    rows_x = jnp.concatenate([got[0][:, :width], got[1][:, :width], got[0][:, width:], got[1][:, width:]], 1)
    rows_g = jnp.concatenate([jnp.where(flip, got[1], got[0]), jnp.where(flip, got[0], got[1])], 1)
    rows = jnp.where(first, rows_x, rows_g)
    block = jnp.concatenate([output_weight, permute(output_weight, SWAP_LOW)], 0)
    numbers = jnp.pad(slots.astype(BF16), (0, 8 - SLOTS))
    numbers = jnp.broadcast_to(numbers[:, None], (8, block.shape[1]))
    came = permute(jnp.concatenate([block, numbers], 0), SWAP_HIGH)
    near = jnp.concatenate([block, came[:-8]], 1)
    other_slots = came[-8:, 0][:SLOTS].astype(jnp.int32)
    rows, near, tables, other_slots = together((rows, near, tables, other_slots))
    gathered = exchange(jnp.broadcast_to(rows[None], (RING,) + rows.shape), GROUPS_GATHER)

    def pick(which):
        local = which % (RING * own)
        return tables[local // own, local % own]

    high = slots // (RING * own)
    other_high = other_slots // (RING * own)
    give = jnp.where((other_high == xh)[:, None, None], pick(other_slots), 0)
    take = permute(give.reshape(-1, 2 * width), SWAP_HIGH).reshape(give.shape)
    chosen = jnp.where((high == xh)[:, None, None], pick(slots), take).reshape(SLOTS * RANK, 2 * width)

    own_slot = (lax.iota(jnp.int32, tokens)[None, :] // SLOT_LEN) == lax.iota(jnp.int32, SLOTS)[:, None]
    contract = (((1,), (1,)), ((), ()))

    every = lax.dot_general(chosen, pair, contract, preferred_element_type=F32)
    sums = jnp.sum(jnp.where(own_slot[:, None, :], every.reshape(SLOTS, RANK, tokens), 0.0), 0)
    sums = sums + permute(sums, SWAP_LOW)
    near, sums = together((near, sums))
    far = permute(near, SWAP_CORE)
    gathered, sums = together((gathered, sums))
    rank_sums = jnp.sum(exchange(jnp.broadcast_to(sums[None], (RING,) + sums.shape), GROUPS_Z), 0)
    partial_value = product(c.reshape(1), gathered.reshape(RING * half, 4 * width), near, far)
    partial_value, rank_sums = together((partial_value, rank_sums))
    spread = exchange(partial_value.reshape(RING, half, 4 * width), GROUPS_SCATTER)
    total = jnp.sum(spread.astype(F32), 0).astype(BF16)

    ranks = jnp.where(first, rank_sums, SCALE * rank_sums).astype(BF16)

    own_columns = jnp.where(first, chosen[:, :width], chosen[:, width:])
    their_columns = jnp.where(first, chosen[:, width:], chosen[:, :width])
    came = permute(jnp.concatenate([jnp.pad(ranks, ((0, 0), (0, width - tokens))), their_columns], 0), SWAP_CORE)
    other_ranks, other_columns = came[:RANK, :tokens], came[RANK:]
    chosen_down, chosen_up = jnp.where(first, own_columns, other_columns), jnp.where(first, other_columns, own_columns)

    def per_slot(value):
        spread_out = jnp.where(own_slot[:, None, :], value[None], jnp.zeros((), BF16))
        return spread_out.reshape(SLOTS * RANK, tokens)

    middle = per_slot(jnp.where(first, ranks, other_ranks))
    grad_middle = per_slot(jnp.where(first, other_ranks, ranks))

    up_terms = (SCALE * jnp.dot(middle, grad_out, preferred_element_type=F32)).astype(BF16)
    down_terms = jnp.dot(grad_middle, attention_output, preferred_element_type=F32).astype(BF16)
    terms = jnp.stack([down_terms, up_terms]).reshape(2, SLOTS, RANK * width)
    away = permute(terms.reshape(2 * SLOTS * RANK, width), SWAP_HIGH).reshape(terms.shape)
    adapters = lax.iota(jnp.int32, RING * own) + xh * (RING * own)
    hot = jnp.concatenate(
        [(adapters[:, None] == slots[None, :]), (adapters[:, None] == other_slots[None, :])], 1
    ).astype(BF16)
    both = jnp.concatenate([terms, away], 1)
    owned = jnp.einsum("as,ksw->akw", hot, both, preferred_element_type=F32).astype(BF16)
    owned = owned.reshape(RING, own * 2 * RANK, width)

    quarters = total.reshape(half, 2, 2, width)
    halves = total.reshape(half, 2, 2 * width)
    sent = []
    for a in (0, 1):
        forward = jnp.where(flip, halves[:, 1 - a], halves[:, a])
        backward = quarters[:, :, a].reshape(half, 2 * width)
        sent.append(jnp.where(first, forward, backward))
    owned, *sent = together((owned, *sent))
    out = [permute(sent[a], FROM_BLOCKS[a]) for a in (0, 1)]
    grads = jnp.sum(exchange(owned, GROUPS_Y).astype(F32), 0).reshape(own, 2, RANK, width)
    back = jnp.where(first, z >> 2, xl)
    both_halves = jnp.concatenate(
        [jnp.where(back == 0, out[0], out[1]), jnp.where(back == 0, out[1], out[0])], 0
    )
    kept = both_halves[:, :width]
    swapped = permute(both_halves[:, width:], SWAP_CORE)
    base = jnp.where(first, kept, swapped).astype(F32)
    frozen_gradient = jnp.where(first, swapped, kept).astype(F32)

    tokens_first = (((0,), (0,)), ((), ()))
    mixed = base + SCALE * lax.dot_general(middle, chosen_up, tokens_first, preferred_element_type=F32)
    input_gradient = frozen_gradient + lax.dot_general(
        grad_middle, chosen_down, tokens_first, preferred_element_type=F32
    )
    return mixed.astype(BF16), input_gradient.astype(BF16), grads[:, 0], grads[:, 1]


def solution(mesh):
    maps = P("fsdp", None, "tp")
    flat_spec = P("fsdp", "tp")
    return jax.shard_map(
        body,
        mesh=mesh,
        in_specs=(flat_spec, P("tp", "fsdp"), maps, maps, P("fsdp", None), P("fsdp", None), flat_spec),
        out_specs=(flat_spec, flat_spec, maps, maps),
        check_vma=False,
    )
```

```python
import jax
import jax.numpy as jnp
from jax import lax
from jax.experimental import pallas as pl
from jax.experimental.pallas import tpu as pltpu
from jax.sharding import PartitionSpec as P

AXES = ("fsdp", "tp")
SCALE = 2.0
SLOTS = 6
SLOT_LEN = 32
RANK = 16
RING = 8
BF16 = jnp.bfloat16
F32 = jnp.float32


def flat(xh, y, z, xl, c):
    return (xh * RING + y) * 4 * RING + z * 4 + xl * 2 + c


DEVICES = [
    (xh, y, z, xl, c)
    for xh in range(2)
    for y in range(RING)
    for z in range(RING)
    for xl in range(2)
    for c in range(2)
]


def pairs(move):
    return [(flat(*d), flat(*move(*d))) for d in DEVICES]


SWAP_CORE = pairs(lambda xh, y, z, xl, c: (xh, y, z, xl, 1 - c))
SWAP_LOW = pairs(lambda xh, y, z, xl, c: (xh, y, z, 1 - xl, c))
SWAP_HIGH = pairs(lambda xh, y, z, xl, c: (1 - xh, y, z, xl, c))


def to_blocks(a):
    def move(xh, y, z, xl, c):
        if c == 0:
            return (xh, y, z, xl ^ a, c)
        return (xh, (2 * z + xl) % RING, y, a ^ (z >> 2), c)

    return pairs(move)


def from_blocks(a):
    def move(xh, y, z, xl, c):
        if c == 1:
            return (xh, y, z, xl ^ a, c)
        return (xh, (z - y) % RING, 4 * (xl ^ a) + (y >> 1), y & 1, c)

    return pairs(move)


TO_BLOCKS = [to_blocks(a) for a in (0, 1)]
FROM_BLOCKS = [from_blocks(a) for a in (0, 1)]


def along_y(xh, z, xl, c):
    return [flat(xh, k, z, xl, c) for k in range(RING)]


def along_z(xh, y, xl, c, turn=0):
    return [flat(xh, y, (k + turn) % RING, xl, c) for k in range(RING)]


OUTER = [(xh, k, xl) for xh in range(2) for k in range(RING) for xl in range(2)]
GROUPS_Y = [along_y(*o, c) for o in OUTER for c in range(2)]
GROUPS_Z = [along_z(*o, c) for o in OUTER for c in range(2)]
GROUPS_GATHER = [along_y(*o, 0) for o in OUTER] + [along_z(*o, 1) for o in OUTER]
GROUPS_SCATTER = [along_z(*o, 0, o[1]) for o in OUTER] + [along_y(*o, 1) for o in OUTER]


def permute(value, where):
    return lax.ppermute(value, AXES, where)


def exchange(value, groups):
    return lax.all_to_all(value, AXES, 0, 0, axis_index_groups=groups, tiled=True)


together = lax.optimization_barrier


def product_kernel(core_ref, rows_ref, near_ref, far_ref, out_ref):
    half = near_ref.shape[0]

    @pl.when(core_ref[0] == 0)
    def _():
        out_ref[...] = (
            jnp.dot(rows_ref[:, :half], near_ref[...], preferred_element_type=F32)
            + jnp.dot(rows_ref[:, half:], far_ref[...], preferred_element_type=F32)
        ).astype(out_ref.dtype)

    @pl.when(core_ref[0] != 0)
    def _():
        contract = (((1,), (1,)), ((), ()))
        for k, ref in enumerate((near_ref, far_ref)):
            out_ref[:, k * half : (k + 1) * half] = lax.dot_general(
                rows_ref[...], ref[...], contract, preferred_element_type=F32
            ).astype(out_ref.dtype)


def product(core, rows, near, far):
    count, width = rows.shape
    tile = count // 4
    whole = lambda i: (0, 0)
    return pl.pallas_call(
        product_kernel,
        grid=(count // tile,),
        in_specs=[
            pl.BlockSpec(memory_space=pltpu.SMEM),
            pl.BlockSpec((tile, width), lambda i: (i, 0)),
            pl.BlockSpec(near.shape, whole),
            pl.BlockSpec(far.shape, whole),
        ],
        out_specs=pl.BlockSpec((tile, width), lambda i: (i, 0)),
        out_shape=jax.ShapeDtypeStruct((count, width), BF16),
        compiler_params=pltpu.CompilerParams(vmem_limit_bytes=24 * 1024 * 1024),
        cost_estimate=pl.CostEstimate(
            flops=2 * count * width * width, bytes_accessed=4 * count * width + 2 * width * width, transcendentals=0
        ),
    )(core, rows, near, far)


def body(attention_output, output_weight, down_maps, up_maps, adapter_index, lengths, cotangent):
    fsdp, tp = lax.axis_index("fsdp"), lax.axis_index("tp")
    xh, z, xl, c = fsdp // RING, tp // 4, (tp // 2) % 2, tp % 2
    first = c == 0
    tokens, width = attention_output.shape
    half = tokens // 2
    own = down_maps.shape[0]

    slots = adapter_index[0]

    positions = lax.iota(jnp.int32, SLOT_LEN)
    live = (positions[None, :] < lengths[0][:, None]).astype(BF16)
    live = live.reshape(tokens, 1)
    grad_out = cotangent * live
    forward = jnp.concatenate([attention_output, down_maps.reshape(-1, width)], 0)
    backward = jnp.concatenate([cotangent, up_maps.reshape(-1, width)], 0)
    mine = jnp.where(first, forward, backward)
    theirs = permute(jnp.where(first, backward, forward), SWAP_CORE)
    pair = jnp.where(first, jnp.concatenate([mine, theirs], 1), jnp.concatenate([theirs, mine], 1))
    pair, table = pair[:tokens] * jnp.where(first, jnp.ones((), BF16), live), pair[tokens:]

    tables = exchange(jnp.broadcast_to(table[None], (RING,) + table.shape), GROUPS_Y)
    tables = tables.reshape(RING, own, RANK, 2 * width)
    side = jnp.where(first, xl, z >> 2)
    top, bottom = pair[:half], pair[half:]
    got = [
        permute(jnp.where(side == 0, top, bottom), TO_BLOCKS[0]),
        permute(jnp.where(side == 0, bottom, top), TO_BLOCKS[1]),
    ]
    near_rows = permute(output_weight, SWAP_LOW)
    got[0], near_rows, slots = together((got[0], near_rows, slots))
    flip = (xh ^ xl) == 1
    rows_x = jnp.concatenate([got[0][:, :width], got[1][:, :width], got[0][:, width:], got[1][:, width:]], 1)
    rows_g = jnp.concatenate([jnp.where(flip, got[1], got[0]), jnp.where(flip, got[0], got[1])], 1)
    rows = jnp.where(first, rows_x, rows_g)
    block = jnp.concatenate([output_weight, near_rows], 0)
    numbers = jnp.pad(slots.astype(BF16), (0, 8 - SLOTS))
    numbers = jnp.broadcast_to(numbers[:, None], (8, block.shape[1]))
    came = permute(jnp.concatenate([block, numbers], 0), SWAP_HIGH)
    other_slots = came[-8:, 0][:SLOTS].astype(jnp.int32)
    rows, block, tables = together((rows, block, tables))
    near = jnp.concatenate([block, came[:-8]], 1)
    gathered = exchange(jnp.broadcast_to(rows[None], (RING,) + rows.shape), GROUPS_GATHER)

    def pick(which):
        local = which % (RING * own)
        return tables[local // own, local % own]

    high = slots // (RING * own)
    other_high = other_slots // (RING * own)
    give = jnp.where((other_high == xh)[:, None, None], pick(other_slots), 0)
    take = permute(give.reshape(-1, 2 * width), SWAP_HIGH).reshape(give.shape)
    chosen = jnp.where((high == xh)[:, None, None], pick(slots), take).reshape(SLOTS * RANK, 2 * width)

    own_slot = (lax.iota(jnp.int32, tokens)[None, :] // SLOT_LEN) == lax.iota(jnp.int32, SLOTS)[:, None]
    contract = (((1,), (1,)), ((), ()))

    every = lax.dot_general(chosen, pair, contract, preferred_element_type=F32)
    sums = jnp.sum(jnp.where(own_slot[:, None, :], every.reshape(SLOTS, RANK, tokens), 0.0), 0)
    sums = sums + permute(sums, SWAP_LOW)
    near, sums = together((near, sums))
    far = permute(near, SWAP_CORE)
    gathered, sums = together((gathered, sums))
    rank_sums = jnp.sum(exchange(jnp.broadcast_to(sums[None], (RING,) + sums.shape), GROUPS_Z), 0)
    partial_value = product(c.reshape(1), gathered.reshape(RING * half, 4 * width), near, far)
    partial_value, rank_sums = together((partial_value, rank_sums))
    spread = exchange(partial_value.reshape(RING, half, 4 * width), GROUPS_SCATTER)
    total = jnp.sum(spread.astype(F32), 0).astype(BF16)

    ranks = jnp.where(first, rank_sums, SCALE * rank_sums).astype(BF16)

    own_columns = jnp.where(first, chosen[:, :width], chosen[:, width:])
    their_columns = jnp.where(first, chosen[:, width:], chosen[:, :width])
    came = permute(jnp.concatenate([jnp.pad(ranks, ((0, 0), (0, width - tokens))), their_columns], 0), SWAP_CORE)
    other_ranks, other_columns = came[:RANK, :tokens], came[RANK:]
    chosen_down, chosen_up = jnp.where(first, own_columns, other_columns), jnp.where(first, other_columns, own_columns)

    def per_slot(value):
        spread_out = jnp.where(own_slot[:, None, :], value[None], jnp.zeros((), BF16))
        return spread_out.reshape(SLOTS * RANK, tokens)

    middle = per_slot(jnp.where(first, ranks, other_ranks))
    grad_middle = per_slot(jnp.where(first, other_ranks, ranks))

    up_terms = (SCALE * jnp.dot(middle, grad_out, preferred_element_type=F32)).astype(BF16)
    down_terms = jnp.dot(grad_middle, attention_output, preferred_element_type=F32).astype(BF16)
    terms = jnp.stack([down_terms, up_terms]).reshape(2, SLOTS, RANK * width)
    away = permute(terms.reshape(2 * SLOTS * RANK, width), SWAP_HIGH).reshape(terms.shape)
    adapters = lax.iota(jnp.int32, RING * own) + xh * (RING * own)
    hot = jnp.concatenate(
        [(adapters[:, None] == slots[None, :]), (adapters[:, None] == other_slots[None, :])], 1
    ).astype(BF16)
    both = jnp.concatenate([terms, away], 1)
    owned = jnp.einsum("as,ksw->akw", hot, both, preferred_element_type=F32).astype(BF16)
    owned = owned.reshape(RING, own * 2 * RANK, width)

    quarters = total.reshape(half, 2, 2, width)
    halves = total.reshape(half, 2, 2 * width)
    sent = []
    for a in (0, 1):
        forward = jnp.where(flip, halves[:, 1 - a], halves[:, a])
        backward = quarters[:, :, a].reshape(half, 2 * width)
        sent.append(jnp.where(first, forward, backward))
    owned, *sent = together((owned, *sent))
    out = [permute(sent[a], FROM_BLOCKS[a]) for a in (0, 1)]
    grads = jnp.sum(exchange(owned, GROUPS_Y).astype(F32), 0).reshape(own, 2, RANK, width)
    back = jnp.where(first, z >> 2, xl)
    both_halves = jnp.concatenate(
        [jnp.where(back == 0, out[0], out[1]), jnp.where(back == 0, out[1], out[0])], 0
    )
    kept = both_halves[:, :width]
    swapped = permute(both_halves[:, width:], SWAP_CORE)
    base = jnp.where(first, kept, swapped).astype(F32)
    frozen_gradient = jnp.where(first, swapped, kept).astype(F32)

    tokens_first = (((0,), (0,)), ((), ()))
    mixed = base + SCALE * lax.dot_general(middle, chosen_up, tokens_first, preferred_element_type=F32)
    input_gradient = frozen_gradient + lax.dot_general(
        grad_middle, chosen_down, tokens_first, preferred_element_type=F32
    )
    return mixed.astype(BF16), input_gradient.astype(BF16), grads[:, 0], grads[:, 1]


def solution(mesh):
    maps = P("fsdp", None, "tp")
    flat_spec = P("fsdp", "tp")
    return jax.shard_map(
        body,
        mesh=mesh,
        in_specs=(flat_spec, P("tp", "fsdp"), maps, maps, P("fsdp", None), P("fsdp", None), flat_spec),
        out_specs=(flat_spec, flat_spec, maps, maps),
        check_vma=False,
    )
```

```python
import jax
import jax.numpy as jnp
from jax import lax
from jax.experimental import pallas as pl
from jax.experimental.pallas import tpu as pltpu
from jax.sharding import PartitionSpec as P

AXES = ("fsdp", "tp")
SCALE = 2.0
SLOTS = 6
SLOT_LEN = 32
RANK = 16
RING = 8
BF16 = jnp.bfloat16
F32 = jnp.float32


def flat(xh, y, z, xl, c):
    return (xh * RING + y) * 4 * RING + z * 4 + xl * 2 + c


DEVICES = [
    (xh, y, z, xl, c)
    for xh in range(2)
    for y in range(RING)
    for z in range(RING)
    for xl in range(2)
    for c in range(2)
]


def pairs(move):
    return [(flat(*d), flat(*move(*d))) for d in DEVICES]


SWAP_CORE = pairs(lambda xh, y, z, xl, c: (xh, y, z, xl, 1 - c))
SWAP_LOW = pairs(lambda xh, y, z, xl, c: (xh, y, z, 1 - xl, c))
SWAP_HIGH = pairs(lambda xh, y, z, xl, c: (1 - xh, y, z, xl, c))


def to_blocks(a):
    def move(xh, y, z, xl, c):
        if c == 0:
            return (xh, y, z, xl ^ a, c)
        return (xh, (2 * z + xl) % RING, y, a ^ (z >> 2), c)

    return pairs(move)


def from_blocks(a):
    def move(xh, y, z, xl, c):
        if c == 1:
            return (xh, y, z, xl ^ a, c)
        return (xh, (z - y) % RING, 4 * (xl ^ a) + (y >> 1), y & 1, c)

    return pairs(move)


TO_BLOCKS = [to_blocks(a) for a in (0, 1)]
FROM_BLOCKS = [from_blocks(a) for a in (0, 1)]


def along_y(xh, z, xl, c):
    return [flat(xh, k, z, xl, c) for k in range(RING)]


def along_z(xh, y, xl, c, turn=0):
    return [flat(xh, y, (k + turn) % RING, xl, c) for k in range(RING)]


OUTER = [(xh, k, xl) for xh in range(2) for k in range(RING) for xl in range(2)]
GROUPS_Y = [along_y(*o, c) for o in OUTER for c in range(2)]
GROUPS_Z = [along_z(*o, c) for o in OUTER for c in range(2)]
GROUPS_GATHER = [along_y(*o, 0) for o in OUTER] + [along_z(*o, 1) for o in OUTER]
GROUPS_SCATTER = [along_z(*o, 0, o[1]) for o in OUTER] + [along_y(*o, 1) for o in OUTER]


def permute(value, where):
    return lax.ppermute(value, AXES, where)


def exchange(value, groups):
    return lax.all_to_all(value, AXES, 0, 0, axis_index_groups=groups, tiled=True)


together = lax.optimization_barrier


def product_kernel(core_ref, rows_ref, near_ref, far_ref, out_ref):
    half = near_ref.shape[0]

    @pl.when(core_ref[0] == 0)
    def _():
        out_ref[...] = (
            jnp.dot(rows_ref[:, :half], near_ref[...], preferred_element_type=F32)
            + jnp.dot(rows_ref[:, half:], far_ref[...], preferred_element_type=F32)
        ).astype(out_ref.dtype)

    @pl.when(core_ref[0] != 0)
    def _():
        contract = (((1,), (1,)), ((), ()))
        for k, ref in enumerate((near_ref, far_ref)):
            out_ref[:, k * half : (k + 1) * half] = lax.dot_general(
                rows_ref[...], ref[...], contract, preferred_element_type=F32
            ).astype(out_ref.dtype)


def product(core, rows, near, far):
    count, width = rows.shape
    tile = count // 4
    whole = lambda i: (0, 0)
    return pl.pallas_call(
        product_kernel,
        grid=(count // tile,),
        in_specs=[
            pl.BlockSpec(memory_space=pltpu.SMEM),
            pl.BlockSpec((tile, width), lambda i: (i, 0)),
            pl.BlockSpec(near.shape, whole),
            pl.BlockSpec(far.shape, whole),
        ],
        out_specs=pl.BlockSpec((tile, width), lambda i: (i, 0)),
        out_shape=jax.ShapeDtypeStruct((count, width), BF16),
        compiler_params=pltpu.CompilerParams(vmem_limit_bytes=24 * 1024 * 1024),
        cost_estimate=pl.CostEstimate(
            flops=2 * count * width * width, bytes_accessed=4 * count * width + 2 * width * width, transcendentals=0
        ),
    )(core, rows, near, far)


def body(attention_output, output_weight, down_maps, up_maps, adapter_index, lengths, cotangent):
    fsdp, tp = lax.axis_index("fsdp"), lax.axis_index("tp")
    xh, z, xl, c = fsdp // RING, tp // 4, (tp // 2) % 2, tp % 2
    first = c == 0
    tokens, width = attention_output.shape
    half = tokens // 2
    own = down_maps.shape[0]

    slots = adapter_index[0]

    positions = lax.iota(jnp.int32, SLOT_LEN)
    live = (positions[None, :] < lengths[0][:, None]).astype(BF16)
    live = live.reshape(tokens, 1)
    grad_out = cotangent * live
    forward = jnp.concatenate([attention_output, down_maps.reshape(-1, width)], 0)
    backward = jnp.concatenate([cotangent, up_maps.reshape(-1, width)], 0)
    mine = jnp.where(first, forward, backward)
    theirs = permute(jnp.where(first, backward, forward), SWAP_CORE)
    pair = jnp.where(first, jnp.concatenate([mine, theirs], 1), jnp.concatenate([theirs, mine], 1))
    pair, table = pair[:tokens] * jnp.where(first, jnp.ones((), BF16), live), pair[tokens:]

    tables = exchange(jnp.broadcast_to(table[None], (RING,) + table.shape), GROUPS_Y)
    tables = tables.reshape(RING, own, RANK, 2 * width)
    side = jnp.where(first, xl, z >> 2)
    top, bottom = pair[:half], pair[half:]
    got = [
        permute(jnp.where(side == 0, top, bottom), TO_BLOCKS[0]),
        permute(jnp.where(side == 0, bottom, top), TO_BLOCKS[1]),
    ]
    near_rows = permute(output_weight, SWAP_LOW)
    got[0], near_rows, slots = together((got[0], near_rows, slots))
    flip = (xh ^ xl) == 1
    rows_x = jnp.concatenate([got[0][:, :width], got[1][:, :width], got[0][:, width:], got[1][:, width:]], 1)
    rows_g = jnp.concatenate([jnp.where(flip, got[1], got[0]), jnp.where(flip, got[0], got[1])], 1)
    rows = jnp.where(first, rows_x, rows_g)
    block = jnp.concatenate([output_weight, near_rows], 0)
    numbers = jnp.pad(slots.astype(BF16), (0, 8 - SLOTS))
    numbers = jnp.broadcast_to(numbers[:, None], (8, block.shape[1]))
    came = permute(jnp.concatenate([block, numbers], 0), SWAP_HIGH)
    other_slots = came[-8:, 0][:SLOTS].astype(jnp.int32)
    rows, block, tables = together((rows, block, tables))
    near = jnp.concatenate([block, came[:-8]], 1)
    gathered = exchange(jnp.broadcast_to(rows[None], (RING,) + rows.shape), GROUPS_GATHER)

    def pick(which):
        local = which % (RING * own)
        return tables[local // own, local % own]

    high = slots // (RING * own)
    other_high = other_slots // (RING * own)
    give = jnp.where((other_high == xh)[:, None, None], pick(other_slots), 0)
    take = permute(give.reshape(-1, 2 * width), SWAP_HIGH).reshape(give.shape)
    chosen = jnp.where((high == xh)[:, None, None], pick(slots), take).reshape(SLOTS * RANK, 2 * width)

    own_slot = (lax.iota(jnp.int32, tokens)[None, :] // SLOT_LEN) == lax.iota(jnp.int32, SLOTS)[:, None]
    contract = (((1,), (1,)), ((), ()))

    every = lax.dot_general(chosen, pair, contract, preferred_element_type=F32)
    sums = jnp.sum(jnp.where(own_slot[:, None, :], every.reshape(SLOTS, RANK, tokens), 0.0), 0)
    sums = sums + permute(sums, SWAP_LOW)
    near, sums = together((near, sums))
    far = permute(near, SWAP_CORE)
    gathered, sums = together((gathered, sums))
    sums = sums.astype(BF16)
    rank_sums = exchange(jnp.broadcast_to(sums[None], (RING,) + sums.shape), GROUPS_Z)
    partial_value = product(c.reshape(1), gathered.reshape(RING * half, 4 * width), near, far)
    partial_value, rank_sums = together((partial_value, rank_sums))
    rank_sums = jnp.sum(rank_sums.astype(F32), 0)
    spread = exchange(partial_value.reshape(RING, half, 4 * width), GROUPS_SCATTER)
    total = jnp.sum(spread.astype(F32), 0).astype(BF16)

    ranks = jnp.where(first, rank_sums, SCALE * rank_sums).astype(BF16)

    own_columns = jnp.where(first, chosen[:, :width], chosen[:, width:])
    their_columns = jnp.where(first, chosen[:, width:], chosen[:, :width])
    came = permute(jnp.concatenate([jnp.pad(ranks, ((0, 0), (0, width - tokens))), their_columns], 0), SWAP_CORE)
    other_ranks, other_columns = came[:RANK, :tokens], came[RANK:]
    chosen_down, chosen_up = jnp.where(first, own_columns, other_columns), jnp.where(first, other_columns, own_columns)

    def per_slot(value):
        spread_out = jnp.where(own_slot[:, None, :], value[None], jnp.zeros((), BF16))
        return spread_out.reshape(SLOTS * RANK, tokens)

    middle = per_slot(jnp.where(first, ranks, other_ranks))
    grad_middle = per_slot(jnp.where(first, other_ranks, ranks))

    up_terms = (SCALE * jnp.dot(middle, grad_out, preferred_element_type=F32)).astype(BF16)
    down_terms = jnp.dot(grad_middle, attention_output, preferred_element_type=F32).astype(BF16)
    terms = jnp.stack([down_terms, up_terms]).reshape(2, SLOTS, RANK * width)
    away = permute(terms.reshape(2 * SLOTS * RANK, width), SWAP_HIGH).reshape(terms.shape)
    adapters = lax.iota(jnp.int32, RING * own) + xh * (RING * own)
    hot = jnp.concatenate(
        [(adapters[:, None] == slots[None, :]), (adapters[:, None] == other_slots[None, :])], 1
    ).astype(BF16)
    both = jnp.concatenate([terms, away], 1)
    owned = jnp.einsum("as,ksw->akw", hot, both, preferred_element_type=F32).astype(BF16)
    owned = owned.reshape(RING, own * 2 * RANK, width)

    quarters = total.reshape(half, 2, 2, width)
    halves = total.reshape(half, 2, 2 * width)
    sent = []
    for a in (0, 1):
        forward = jnp.where(flip, halves[:, 1 - a], halves[:, a])
        backward = quarters[:, :, a].reshape(half, 2 * width)
        sent.append(jnp.where(first, forward, backward))
    owned, *sent = together((owned, *sent))
    out = [permute(sent[a], FROM_BLOCKS[a]) for a in (0, 1)]
    grads = jnp.sum(exchange(owned, GROUPS_Y).astype(F32), 0).reshape(own, 2, RANK, width)
    back = jnp.where(first, z >> 2, xl)
    both_halves = jnp.concatenate(
        [jnp.where(back == 0, out[0], out[1]), jnp.where(back == 0, out[1], out[0])], 0
    )
    kept = both_halves[:, :width]
    swapped = permute(both_halves[:, width:], SWAP_CORE)
    base = jnp.where(first, kept, swapped).astype(F32)
    frozen_gradient = jnp.where(first, swapped, kept).astype(F32)

    tokens_first = (((0,), (0,)), ((), ()))
    mixed = base + SCALE * lax.dot_general(middle, chosen_up, tokens_first, preferred_element_type=F32)
    input_gradient = frozen_gradient + lax.dot_general(
        grad_middle, chosen_down, tokens_first, preferred_element_type=F32
    )
    return mixed.astype(BF16), input_gradient.astype(BF16), grads[:, 0], grads[:, 1]


def solution(mesh):
    maps = P("fsdp", None, "tp")
    flat_spec = P("fsdp", "tp")
    return jax.shard_map(
        body,
        mesh=mesh,
        in_specs=(flat_spec, P("tp", "fsdp"), maps, maps, P("fsdp", None), P("fsdp", None), flat_spec),
        out_specs=(flat_spec, flat_spec, maps, maps),
        check_vma=False,
    )
```
